256 devices in a mesh: node: 32 (over x, y, core), outer: 8 (over z).
Axes of the slice: x: 4, y: 4, z: 8, core: 2. Of those that a mesh axis runs over, the one named last changes fastest.
Arguments:
- acts: bfloat16 [81920, 14336], P(('node', 'outer')), may hold values from -6 to 6
- cotangent: bfloat16 [81920, 128], P(('node', 'outer')), may hold values from -24 to 24
- signs: int32 [56, 256], replicated, may hold values from -1 to 1, as said below
Outputs:
- rotated_mean: float32 [7168, 256], P(('node', 'outer'))
- grad_mean: bfloat16 [7168, 256], replicated
The draws below stay inside these ranges and needn't reach their ends.
Inputs may be any that keep to these rules, and one draw needn't show every extreme that they name: `signs`: every entry is -1 or 1.
All inputs are finite; a program needn't handle non-finite values.
Results may differ from the reference program's by a relative error of at most 0.012.
Values may be sent and summed in bfloat16 or wider, within the bound.
No kernel may reach another device: no remote copies, remote signals or barrier semaphores. Data moves between devices by JAX's collectives and lax.ppermute only.
A program may use at most 128 MiB of HBM per device.

```python
import math
import jax
import jax.numpy as jnp
from jax import lax

D = 14336
COLS = 128
BLK = 256
LEVELS = 15
TOK_DEV = 320
BLOCKS = 56
TOKENS = 81920
N_NODE = 32
N_OUTER = 8


def draw_signs(key, part):
    key = jax.random.fold_in(key, 1)
    return (2 * jax.random.randint(key, (BLOCKS, BLK), 0, 2) - 1).astype(jnp.int32)


def spiked(array, rng, source, target, parts, factor):
    def block_of(axis_at):
        return (jnp.arange(array.shape[axis_at]) // (array.shape[axis_at] // parts)).reshape((-1,) + (1,) * (array.ndim - 1 - axis_at))

    first = jax.random.permutation(rng, parts)[block_of(target)]
    other_side = (block_of(target) + parts // 2) % parts
    return jnp.where((block_of(source) == first) | (block_of(source) == other_side), factor * array, array)


def block_levels(own_key, shape, split, least, top_value):
    def one(dim, parts):
        steps = jax.random.uniform(jax.random.fold_in(jax.random.fold_in(own_key, 6), dim), (parts,), jnp.float32, least / len(split), top_value / len(split))
        return jnp.repeat(jnp.exp(steps), shape[dim] // parts).reshape((-1,) + (1,) * (len(shape) - dim - 1))

    level = one(*split[0])
    for cut in split[1:]:
        level = level * one(*cut)
    return level


def noise(rng, dims, scale, limit, pieces=(), kind=jnp.bfloat16):
    drawn = jax.random.normal(rng, dims, jnp.float32) * scale
    if len(pieces) > 0:
        drawn = block_levels(rng, dims, pieces, -0.22, 0.18) * drawn
    return jnp.clip(drawn, min=-limit, max=limit).astype(kind)


def heavy_noise(key, shape, scale, reach, pieces, heavy, kind=jnp.bfloat16):
    values = scale * jax.random.normal(key, shape, jnp.float32)
    if pieces:
        values = values * block_levels(key, shape, pieces, -0.22, 0.18)
    return jnp.clip(spiked(values, jax.random.fold_in(key, 3), *heavy), -reach, reach).astype(kind)


def setup_inputs(seed: int = 0) -> dict:
    key_list = jax.random.split(jax.random.key(seed), 4)
    acts = noise(key_list[0], (TOKENS, D), 1.0, 6.0, ((0, 256),))
    cotangent = heavy_noise(key_list[1], (TOKENS, COLS), 1.0, 24.0, ((0, 256),), (0, 1, 128, 5.5))
    signs = draw_signs(jax.random.fold_in(key_list[3], 71), 0)
    return dict(acts=acts, cotangent=cotangent, signs=signs)


def hadamard(size):
    index = jnp.arange(size, dtype=jnp.int32)
    parity = jnp.zeros((size, size), jnp.int32)
    bit = 1
    while bit < size:
        parity = parity + index[:, None] // bit % 2 * (index[None, :] // bit % 2)
        bit = bit * 2
    return jnp.where(parity % 2 == 0, 1.0, -1.0).astype(jnp.float32)

def rotate(partial_value, signs):
    blocks = partial_value.reshape(BLOCKS, BLK, COLS) * signs.astype(jnp.float32)[:, :, None]
    turned = jnp.einsum('ij,bjc->bci', hadamard(BLK), blocks, precision=lax.Precision.HIGHEST)
    return (turned * (1.0 / math.sqrt(BLK))).reshape(BLOCKS * COLS, BLK)

def reference(acts, cotangent, signs):
    devices = N_NODE * N_OUTER
    xs = acts.reshape(devices, TOK_DEV, D)
    gs = cotangent.reshape(devices, TOK_DEV, COLS)

    def local(x, g):
        partial_value = lax.dot_general(x, g, (((0,), (0,)), ((), ())), preferred_element_type=jnp.float32)
        return rotate(partial_value, signs)

    def find_max(carry, pair):
        turned = local(pair[0], pair[1])
        return (jnp.maximum(carry, lax.optimization_barrier(jnp.max(jnp.abs(turned), axis=1))), None)
    largest, _ = lax.scan(find_max, jnp.zeros((BLOCKS * COLS,), jnp.float32), (xs, gs))
    scale = largest + 1e-06

    def add_quant(carry, pair):
        turned = local(pair[0], pair[1])
        return (carry + jnp.floor(turned / scale[:, None] * LEVELS + 0.5), None)
    total, _ = lax.scan(add_quant, jnp.zeros((BLOCKS * COLS, BLK), jnp.float32), (xs, gs))
    rotated_mean = total * scale[:, None] / (LEVELS * devices)
    sign_rows = jnp.repeat(signs.astype(jnp.float32), COLS, axis=0)
    back = jnp.dot(rotated_mean, hadamard(BLK), precision=lax.Precision.HIGHEST)
    grad_mean = (back * sign_rows * (1.0 / math.sqrt(BLK))).astype(jnp.bfloat16)
    return (rotated_mean, grad_mean)
```

```python
import math

import jax
import jax.numpy as jnp
from jax import lax
from jax.sharding import Mesh
from jax.sharding import PartitionSpec as P

COLS = 128
BLK = 256
LEVELS = 15
BLOCKS = 56
NX = 4
NY = 4
NZ = 8
HALF = 112
DEVICES = 256


def hadamard(size):
    index = jnp.arange(size, dtype=jnp.int32)
    parity = jnp.zeros((size, size), jnp.int32)
    bit = 1
    while bit < size:
        parity = parity + index[:, None] // bit % 2 * (index[None, :] // bit % 2)
        bit = bit * 2
    return jnp.where(parity % 2 == 0, 1.0, -1.0).astype(jnp.float32)


def rotate(partial_value, signs):
    blocks = partial_value.reshape(BLOCKS, BLK, COLS) * signs.astype(jnp.float32)[:, :, None]
    turned = jnp.einsum("ij,bjc->bci", hadamard(BLK), blocks, precision=lax.Precision.HIGHEST)
    return (turned * (1.0 / math.sqrt(BLK))).reshape(BLOCKS * COLS, BLK)


def row_signs(signs, first_row, count):
    row_ids = first_row + jnp.arange(count, dtype=jnp.int32)
    onehot = (row_ids[:, None] // COLS == jnp.arange(BLOCKS, dtype=jnp.int32)[None, :]).astype(
        jnp.float32
    )
    return jnp.dot(onehot, signs.astype(jnp.float32), precision=lax.Precision.HIGHEST)


def unrotate(values, signs, first_row):
    back = jnp.dot(values, hadamard(BLK), precision=lax.Precision.HIGHEST)
    signed = back * row_signs(signs, first_row, values.shape[0])
    return (signed * (1.0 / math.sqrt(BLK))).astype(jnp.bfloat16)


def shift(value, axis, size, step):
    return lax.ppermute(value, axis, [((i + step) % size, i) for i in range(size)])


def flip(value, axis, size, bit):
    return lax.ppermute(value, axis, [(i, i ^ bit) for i in range(size)])


def max_everywhere(value):
    value = jnp.maximum(value, flip(value, "c", 2, 1))
    for axis, size, steps in (
        ("x", NX, (1, 2, 3)),
        ("y", NY, (1, 2, 3)),
        ("z", NZ, (1, 7)),
        ("z", NZ, (3, 5)),
    ):
        got = [shift(value, axis, size, s) for s in steps]
        for g in got:
            value = jnp.maximum(value, g)
    return value


def scatter_sum(value, axis, dim):
    size = value.shape[dim]
    me = lax.axis_index(axis)

    def part(i):
        return lax.dynamic_index_in_dim(value, i, dim, keepdims=False)

    total = part(me).astype(jnp.float32)
    for s in range(1, size):
        got = shift(part((me - s) % size), axis, size, s)
        total = total + got.astype(jnp.float32)
    return total.astype(jnp.bfloat16)


def gather(value, axis, size, dim):
    me = lax.axis_index(axis)
    parts = [value] + [shift(value, axis, size, s) for s in range(1, size)]
    twice = jnp.stack(parts + parts, axis=dim)
    return lax.dynamic_slice_in_dim(twice, (size - me) % size, size, dim)


def body(acts, cotangent, signs):
    x, y, c, z = (lax.axis_index(a) for a in ("x", "y", "c", "z"))
    partial_value = lax.dot_general(
        acts, cotangent, (((0,), (0,)), ((), ())), preferred_element_type=jnp.float32
    )
    turned = rotate(partial_value, signs)
    largest = jnp.max(jnp.abs(turned), axis=1).reshape(BLOCKS, COLS)
    scale = max_everywhere(largest).reshape(BLOCKS * COLS) + 1e-06
    quant = jnp.floor(turned / scale[:, None] * LEVELS + 0.5).astype(jnp.bfloat16)
    quant = quant.reshape(NX, NY, 2, 2, HALF, BLK)
    means = []
    grads = []
    for k in range(2):
        mine = quant[:, :, :, k]
        keep = lax.dynamic_index_in_dim(mine, c, 2, keepdims=False)
        give = lax.dynamic_index_in_dim(mine, 1 - c, 2, keepdims=False)
        value = keep + flip(give, "c", 2, 1)
        if k == 0:
            value = scatter_sum(scatter_sum(value, "x", 0), "y", 0)
        else:
            value = scatter_sum(scatter_sum(value, "y", 1), "x", 0)
        for bit in (1, 2, 4):
            value = value + flip(value, "z", NZ, bit)
        first_row = ((x * NY + y) * 2 + c) * (2 * HALF) + k * HALF
        own_scale = lax.dynamic_slice_in_dim(scale, first_row, HALF, 0)
        mean = value.astype(jnp.float32) * own_scale[:, None] / (LEVELS * DEVICES)
        grad = unrotate(mean, signs, first_row)
        if k == 0:
            grad = gather(gather(grad, "y", NY, 0), "x", NX, 0)
        else:
            grad = gather(gather(grad, "x", NX, 0), "y", NY, 1)
        other = flip(grad, "c", 2, 1)
        first = jnp.where(c == 0, grad, other)
        second = jnp.where(c == 0, other, grad)
        means.append(mean)
        grads.append(jnp.stack([first, second], axis=2))
    mean = jnp.concatenate(means, axis=0)
    rotated_mean = lax.dynamic_slice_in_dim(mean, z * 28, 28, 0)
    grad_mean = jnp.stack(grads, axis=3).reshape(BLOCKS * COLS, BLK)
    return (rotated_mean, grad_mean)


def solution(mesh):
    fine = Mesh(mesh.devices.reshape(NX, NY, 2, NZ), ("x", "y", "c", "z"))
    rows = ("x", "y", "c", "z")
    in_specs = (P(rows, None), P(rows, None), P())
    out_specs = (P(rows, None), P())
    return jax.shard_map(body, mesh=fine, in_specs=in_specs, out_specs=out_specs, check_vma=False)
```

```python
import math

import jax
import jax.numpy as jnp
import numpy as np
from jax import lax
from jax.experimental import pallas as pl
from jax.experimental.pallas import tpu as pltpu
from jax.sharding import Mesh
from jax.sharding import PartitionSpec as P

COLS = 128
BLK = 256
LEVELS = 15
BLOCKS = 56
ROWS = BLOCKS * COLS
NX = 4
NY = 4
NZ = 8
PLANE = NX * NY
DEVICES = 256
CORE_ROWS = ROWS // (2 * PLANE)
OWN = ROWS // DEVICES
GROUP = 7
STEPS = BLOCKS // GROUP
PAIRS = PLANE // STEPS
VMEM_BYTES = 48 * 1024 * 1024


def hadamard(size):
    matrix = np.ones((1, 1), np.float32)
    while matrix.shape[0] < size:
        matrix = np.block([[matrix, matrix], [matrix, -matrix]])
    return matrix


HADAMARD = hadamard(BLK)


def rotate_kernel(core_ref, acts_ref, cot_ref, signs_ref, had_ref, keep_ref, give_ref, largest_ref, cot_t, turned_ref):
    step = pl.program_id(0)
    core = core_ref[0]

    @pl.when(step == 0)
    def _():
        cot_t[...] = cot_ref[...].T

    for b in range(GROUP):
        block = jnp.dot(
            cot_t[...], acts_ref[:, b * BLK : (b + 1) * BLK], preferred_element_type=jnp.float32
        )
        row = pl.ds(step * GROUP + b, 1)
        block = block * signs_ref[row, :].astype(jnp.float32)
        high = block.astype(jnp.bfloat16)
        low = (block - high.astype(jnp.float32)).astype(jnp.bfloat16)
        had = had_ref[...]
        turned = jnp.dot(high, had, preferred_element_type=jnp.float32)
        turned = turned + jnp.dot(low, had, preferred_element_type=jnp.float32)
        turned = turned * (1.0 / math.sqrt(BLK))
        turned_ref[b * COLS : (b + 1) * COLS, :] = turned
        size = jnp.abs(turned)
        size = jnp.maximum(size[:, :COLS], size[:, COLS:]).T
        largest_ref[row, :] = jnp.max(size, axis=0, keepdims=True)
    for pair in range(PAIRS):
        for ref, part in ((keep_ref, core), (give_ref, 1 - core)):
            start = pl.multiple_of((2 * pair + part) * CORE_ROWS, 8)
            ref[pair] = turned_ref[pl.ds(start, CORE_ROWS), :]


def rotate(core, acts, cotangent, signs, had):
    tokens = acts.shape[0]
    half = jax.ShapeDtypeStruct((PLANE, CORE_ROWS, BLK), jnp.float32)
    out_spec = pl.BlockSpec((PAIRS, CORE_ROWS, BLK), lambda i, core: (i, 0, 0))
    return pl.pallas_call(
        rotate_kernel,
        grid_spec=pltpu.PrefetchScalarGridSpec(
            num_scalar_prefetch=1,
            grid=(STEPS,),
            in_specs=[
                pl.BlockSpec((tokens, GROUP * BLK), lambda i, core: (0, i)),
                pl.BlockSpec((tokens, COLS), lambda i, core: (0, 0)),
                pl.BlockSpec((BLOCKS, BLK), lambda i, core: (0, 0)),
                pl.BlockSpec((BLK, BLK), lambda i, core: (0, 0)),
            ],
            out_specs=[
                out_spec,
                out_spec,
                pl.BlockSpec((BLOCKS, COLS), lambda i, core: (0, 0)),
            ],
            scratch_shapes=[
                pltpu.VMEM((COLS, tokens), jnp.bfloat16),
                pltpu.VMEM((GROUP * COLS, BLK), jnp.float32),
            ],
        ),
        out_shape=[half, half, jax.ShapeDtypeStruct((BLOCKS, COLS), jnp.float32)],
        compiler_params=pltpu.CompilerParams(vmem_limit_bytes=VMEM_BYTES),
        cost_estimate=pl.CostEstimate(
            flops=2 * ROWS * BLK * (tokens + 2 * BLK), bytes_accessed=17_000_000, transcendentals=0
        ),
    )(core, acts, cotangent, signs, had)


def quantize_kernel(core_ref, keep_ref, other_ref, scale_ref, sum_ref, factor):
    core = core_ref[0]
    first = pl.program_id(0) * GROUP
    for b in range(GROUP):
        row = LEVELS / scale_ref[pl.ds(first + b, 1), :]
        factor[b * COLS : (b + 1) * COLS, :] = jnp.broadcast_to(row, (COLS, COLS)).T
    for pair in range(PAIRS):
        start = pl.multiple_of((2 * pair + core) * CORE_ROWS, 8)
        scale = factor[pl.ds(start, CORE_ROWS), :]
        for lane in (0, COLS):
            mine = jnp.floor(keep_ref[pair, :, lane : lane + COLS] * scale + 0.5)
            other = jnp.floor(other_ref[pair, :, lane : lane + COLS] * scale + 0.5)
            sum_ref[pair, :, lane : lane + COLS] = (mine + other).astype(jnp.bfloat16)


def quantize(core, keep, other, scale):
    spec = pl.BlockSpec((PAIRS, CORE_ROWS, BLK), lambda i, core: (i, 0, 0))
    return pl.pallas_call(
        quantize_kernel,
        grid_spec=pltpu.PrefetchScalarGridSpec(
            num_scalar_prefetch=1,
            grid=(STEPS,),
            in_specs=[spec, spec, pl.BlockSpec((BLOCKS, COLS), lambda i, core: (0, 0))],
            out_specs=spec,
            scratch_shapes=[pltpu.VMEM((GROUP * COLS, COLS), jnp.float32)],
        ),
        out_shape=jax.ShapeDtypeStruct((PLANE, CORE_ROWS, BLK), jnp.bfloat16),
        compiler_params=pltpu.CompilerParams(vmem_limit_bytes=VMEM_BYTES),
        cost_estimate=pl.CostEstimate(
            flops=4 * ROWS * BLK, bytes_accessed=9_200_000, transcendentals=0
        ),
    )(core, keep, other, scale)


def row_signs(signs, first_row, count):
    row_ids = first_row + jnp.arange(count, dtype=jnp.int32)
    onehot = (row_ids[:, None] // COLS == jnp.arange(BLOCKS, dtype=jnp.int32)[None, :]).astype(
        jnp.float32
    )
    return jnp.dot(onehot, signs.astype(jnp.float32), precision=lax.Precision.HIGHEST)


def unrotate(values, signs, first_row):
    back = jnp.dot(values, jnp.asarray(HADAMARD), precision=lax.Precision.HIGHEST)
    signed = back * row_signs(signs, first_row, values.shape[0])
    return (signed * (1.0 / math.sqrt(BLK))).astype(jnp.bfloat16)


def shift(value, axis, size, step):
    return lax.ppermute(value, axis, [((i + step) % size, i) for i in range(size)])


def flip(value, axis, size, bit):
    return lax.ppermute(value, axis, [(i, i ^ bit) for i in range(size)])


def max_everywhere(value):
    value = jnp.maximum(value, flip(value, "c", 2, 1))
    for axis, size, steps in (
        ("x", NX, (1, 2, 3)),
        ("y", NY, (1, 2, 3)),
        ("z", NZ, (1, 7)),
        ("z", NZ, (3, 5)),
    ):
        got = [shift(value, axis, size, s) for s in steps]
        for g in got:
            value = jnp.maximum(value, g)
    return value


def body(acts, cotangent, signs):
    x, y, c, z = (lax.axis_index(a) for a in ("x", "y", "c", "z"))
    core = jnp.full((1,), c, jnp.int32)
    had = jnp.asarray(HADAMARD, jnp.bfloat16)
    keep, give, largest = rotate(core, acts, cotangent, signs, had)
    scale = max_everywhere(largest) + 1e-06
    other = flip(give, "c", 2, 1)
    parts = quantize(core, keep, other, scale)
    parts = lax.all_to_all(parts, ("x", "y"), 0, 0, tiled=True)
    value = jnp.sum(parts.astype(jnp.float32), axis=0).astype(jnp.bfloat16)
    got = [flip(value, "z", NZ, bit) for bit in (1, 2, 3)]
    value = value.astype(jnp.float32)
    for g in got:
        value = value + g.astype(jnp.float32)
    value = value.astype(jnp.bfloat16)
    value = value.astype(jnp.float32) + flip(value, "z", NZ, 4).astype(jnp.float32)
    first_row = ((x * NY + y) * 2 + c) * CORE_ROWS
    own_scale = lax.dynamic_slice_in_dim(scale.reshape(ROWS), first_row, CORE_ROWS, 0)
    mean = value * own_scale[:, None] / (LEVELS * DEVICES)
    rotated_mean = lax.dynamic_slice_in_dim(mean, z * OWN, OWN, 0)
    grad = unrotate(mean, signs, first_row)
    grad = jnp.broadcast_to(grad[None], (PLANE, CORE_ROWS, BLK))
    grad = lax.all_to_all(grad, ("x", "y"), 0, 0, tiled=True)
    other = flip(grad, "c", 2, 1)
    first = jnp.where(c == 0, grad, other)
    second = jnp.where(c == 0, other, grad)
    grad_mean = jnp.stack([first, second], axis=1).reshape(ROWS, BLK)
    return (rotated_mean, grad_mean)


def solution(mesh):
    fine = Mesh(mesh.devices.reshape(NX, NY, 2, NZ), ("x", "y", "c", "z"))
    rows = ("x", "y", "c", "z")
    in_specs = (P(rows, None), P(rows, None), P())
    out_specs = (P(rows, None), P())
    return jax.shard_map(body, mesh=fine, in_specs=in_specs, out_specs=out_specs, check_vma=False)
```

```python
import math

import jax
import jax.numpy as jnp
import numpy as np
from jax import lax
from jax.experimental import pallas as pl
from jax.experimental.pallas import tpu as pltpu
from jax.sharding import Mesh
from jax.sharding import PartitionSpec as P

COLS = 128
BLK = 256
LEVELS = 15
BLOCKS = 56
ROWS = BLOCKS * COLS
NX = 4
NY = 4
NZ = 8
PLANE = NX * NY
DEVICES = 256
CORE_ROWS = ROWS // (2 * PLANE)
OWN = ROWS // DEVICES
GROUP = 7
STEPS = BLOCKS // GROUP
PAIRS = PLANE // STEPS
WIDTH = GROUP * BLK
AHEAD = 3
ROTATE_VMEM = 44 * 1024 * 1024
KERNEL_VMEM = 24 * 1024 * 1024
IN_VMEM = pl.BlockSpec(memory_space=pltpu.VMEM)
IN_SMEM = pl.BlockSpec(memory_space=pltpu.SMEM)
IN_ANY = pl.BlockSpec(memory_space=pl.ANY)


def hadamard(size):
    matrix = np.ones((1, 1), np.float32)
    while matrix.shape[0] < size:
        matrix = np.block([[matrix, matrix], [matrix, -matrix]])
    return matrix


HADAMARD = hadamard(BLK)


def rotate_kernel(
    core_ref,
    acts_hbm,
    cot_hbm,
    signs_hbm,
    keep_ref,
    give_ref,
    largest_ref,
    acts_ref,
    cot_ref,
    signs_ref,
    had_ref,
    cot_t,
    even_terms,
    odd_terms,
    turned_ref,
    sems,
    small_sems,
):
    core = core_ref[0]
    small = [
        pltpu.make_async_copy(source, target, small_sems.at[i])
        for i, (source, target) in enumerate(((cot_hbm, cot_ref), (signs_hbm, signs_ref)))
    ]

    def fetch(i):
        columns = pl.ds(pl.multiple_of(i * WIDTH, WIDTH), WIDTH)
        return pltpu.make_async_copy(acts_hbm.at[:, columns], acts_ref.at[i], sems.at[i])

    for copy in small:
        copy.start()
    for i in range(AHEAD):
        fetch(i).start()
    had = lax.broadcasted_iota(jnp.int32, (BLK, BLK), 0) & lax.broadcasted_iota(
        jnp.int32, (BLK, BLK), 1
    )
    for half in (4, 2, 1):
        had = had ^ (had >> half)
    had = (1 - 2 * (had & 1)).astype(jnp.float32) * (1.0 / math.sqrt(BLK))
    had = had.astype(jnp.bfloat16)
    had_ref[:BLK, :] = had
    had_ref[BLK:, :] = had
    for copy in small:
        copy.wait()
    cot_t[...] = cot_ref[...].T

    def arrive(i):
        fetch(i).wait()

        @pl.when(i + AHEAD < STEPS)
        def _():
            fetch(i + AHEAD).start()

    def multiply(i, b, terms):
        block = jnp.dot(
            cot_t[...], acts_ref[i, :, b * BLK : (b + 1) * BLK], preferred_element_type=jnp.float32
        )
        block = block * signs_ref[pl.ds(i * GROUP + b, 1), :].astype(jnp.float32)
        high = block.astype(jnp.bfloat16)
        low = (block - high.astype(jnp.float32)).astype(jnp.bfloat16)
        terms[b * COLS : (b + 1) * COLS, :BLK] = high
        terms[b * COLS : (b + 1) * COLS, BLK:] = low

    def turn(i, b, terms):
        turned = jnp.dot(
            terms[b * COLS : (b + 1) * COLS, :], had_ref[...], preferred_element_type=jnp.float32
        )
        turned_ref[b * COLS : (b + 1) * COLS, :] = turned
        size = jnp.abs(turned)
        size = jnp.maximum(size[:, :COLS], size[:, COLS:]).T
        largest_ref[pl.ds(i * GROUP + b, 1), :] = jnp.max(size, axis=0, keepdims=True)

    def hand_out(i):
        for pair in range(PAIRS):
            for ref, part in ((keep_ref, core), (give_ref, 1 - core)):
                start = pl.multiple_of((2 * pair + part) * CORE_ROWS, 8)
                ref[i * PAIRS + pair] = turned_ref[pl.ds(start, CORE_ROWS), :]

    def both(i, terms, next_terms):
        arrive(i + 1)
        for b in range(GROUP):
            multiply(i + 1, b, next_terms)
            turn(i, b, terms)
        hand_out(i)

    arrive(0)
    for b in range(GROUP):
        multiply(0, b, even_terms)

    def two_steps(k, carry):
        both(2 * k, even_terms, odd_terms)
        both(2 * k + 1, odd_terms, even_terms)
        return carry

    lax.fori_loop(0, STEPS // 2 - 1, two_steps, 0)
    both(STEPS - 2, even_terms, odd_terms)
    for b in range(GROUP):
        turn(STEPS - 1, b, odd_terms)
    hand_out(STEPS - 1)


def rotate(core, acts, cotangent, signs):
    tokens = acts.shape[0]
    half = jax.ShapeDtypeStruct((PLANE, CORE_ROWS, BLK), jnp.float32)
    return pl.pallas_call(
        rotate_kernel,
        in_specs=[IN_SMEM, IN_ANY, IN_ANY, IN_ANY],
        out_specs=[IN_VMEM, IN_VMEM, IN_VMEM],
        out_shape=[half, half, jax.ShapeDtypeStruct((BLOCKS, COLS), jnp.float32)],
        scratch_shapes=[
            pltpu.VMEM((STEPS, tokens, WIDTH), jnp.bfloat16),
            pltpu.VMEM((tokens, COLS), jnp.bfloat16),
            pltpu.VMEM((BLOCKS, BLK), jnp.int32),
            pltpu.VMEM((2 * BLK, BLK), jnp.bfloat16),
            pltpu.VMEM((COLS, tokens), jnp.bfloat16),
            pltpu.VMEM((GROUP * COLS, 2 * BLK), jnp.bfloat16),
            pltpu.VMEM((GROUP * COLS, 2 * BLK), jnp.bfloat16),
            pltpu.VMEM((GROUP * COLS, BLK), jnp.float32),
            pltpu.SemaphoreType.DMA((STEPS,)),
            pltpu.SemaphoreType.DMA((2,)),
        ],
        compiler_params=pltpu.CompilerParams(vmem_limit_bytes=ROTATE_VMEM),
        cost_estimate=pl.CostEstimate(
            flops=2 * ROWS * BLK * (tokens + 2 * BLK), bytes_accessed=17_000_000, transcendentals=0
        ),
    )(core, acts, cotangent, signs)


def quantize_kernel(core_ref, keep_ref, other_ref, scale_ref, sum_ref, factor):
    core = core_ref[0]

    def step(i, carry):
        for b in range(GROUP):
            row = LEVELS / scale_ref[pl.ds(i * GROUP + b, 1), :]
            factor[b * COLS : (b + 1) * COLS, :] = jnp.broadcast_to(row, (COLS, COLS)).T
        for pair in range(PAIRS):
            start = pl.multiple_of((2 * pair + core) * CORE_ROWS, 8)
            scale = factor[pl.ds(start, CORE_ROWS), :]
            j = i * PAIRS + pair
            for lane in (0, COLS):
                mine = jnp.floor(keep_ref[j, :, lane : lane + COLS] * scale + 0.5)
                other = jnp.floor(other_ref[j, :, lane : lane + COLS] * scale + 0.5)
                sum_ref[j, :, lane : lane + COLS] = (mine + other).astype(jnp.bfloat16)
        return carry

    lax.fori_loop(0, STEPS, step, 0)


def quantize(core, keep, other, scale):
    return pl.pallas_call(
        quantize_kernel,
        in_specs=[IN_SMEM, IN_VMEM, IN_VMEM, IN_VMEM],
        out_specs=IN_VMEM,
        out_shape=jax.ShapeDtypeStruct((PLANE, CORE_ROWS, BLK), jnp.bfloat16),
        scratch_shapes=[pltpu.VMEM((GROUP * COLS, COLS), jnp.float32)],
        compiler_params=pltpu.CompilerParams(vmem_limit_bytes=KERNEL_VMEM),
        cost_estimate=pl.CostEstimate(
            flops=4 * ROWS * BLK, bytes_accessed=9_200_000, transcendentals=0
        ),
    )(core, keep, other, scale)


def place_kernel(core_ref, part_ref, whole_ref, sem):
    copies = [
        pltpu.make_async_copy(part_ref.at[i], whole_ref.at[i, core_ref[0]], sem.at[i])
        for i in range(PLANE)
    ]
    for copy in copies:
        copy.start()
    for copy in copies:
        copy.wait()


def place(core, part):
    return pl.pallas_call(
        place_kernel,
        in_specs=[IN_SMEM, IN_VMEM],
        out_specs=IN_ANY,
        out_shape=jax.ShapeDtypeStruct((PLANE, 2, CORE_ROWS, BLK), jnp.bfloat16),
        scratch_shapes=[pltpu.SemaphoreType.DMA((PLANE,))],
        compiler_params=pltpu.CompilerParams(vmem_limit_bytes=KERNEL_VMEM),
        cost_estimate=pl.CostEstimate(flops=0, bytes_accessed=3_700_000, transcendentals=0),
    )(core, part)


def row_signs(signs, first_row, count):
    row_ids = first_row + jnp.arange(count, dtype=jnp.int32)
    onehot = (row_ids[:, None] // COLS == jnp.arange(BLOCKS, dtype=jnp.int32)[None, :]).astype(
        jnp.float32
    )
    return jnp.dot(onehot, signs.astype(jnp.float32), precision=lax.Precision.HIGHEST)


def unrotate(values, signs, first_row):
    back = jnp.dot(values, jnp.asarray(HADAMARD), precision=lax.Precision.HIGHEST)
    signed = back * row_signs(signs, first_row, values.shape[0])
    return (signed * (1.0 / math.sqrt(BLK))).astype(jnp.bfloat16)


def shift(value, axis, size, step):
    return lax.ppermute(value, axis, [((i + step) % size, i) for i in range(size)])


def flip(value, axis, size, bit):
    return lax.ppermute(value, axis, [(i, i ^ bit) for i in range(size)])


def mirror(value, axis, size):
    return lax.ppermute(value, axis, [(i, size - 1 - i) for i in range(size)])


def max_everywhere(value):
    for axis, size, steps in (
        ("x", NX, (1, 2, 3)),
        ("y", NY, (1, 2, 3)),
        ("z", NZ, (1, 7)),
        ("z", NZ, (3, 5)),
    ):
        got = [shift(value, axis, size, s) for s in steps]
        for g in got:
            value = jnp.maximum(value, g)
    return value


def sum_z(value):
    got = [flip(value, "z", NZ, bit) for bit in (1, 2, 3)]
    value = value.astype(jnp.float32)
    for g in got:
        value = value + g.astype(jnp.float32)
    value = value.astype(jnp.bfloat16)
    return value.astype(jnp.float32) + mirror(value, "z", NZ).astype(jnp.float32)


def body(acts, cotangent, signs):
    x, y, c, z = (lax.axis_index(a) for a in ("x", "y", "c", "z"))
    core = jnp.full((1,), c, jnp.int32)
    keep, give, largest = rotate(core, acts, cotangent, signs)
    beside = flip(largest, "c", 2, 1)
    give, beside = lax.optimization_barrier((give, beside))
    other = flip(give, "c", 2, 1)
    scale = max_everywhere(jnp.maximum(largest, beside)) + 1e-06
    parts = quantize(core, keep, other, scale)
    parts = lax.all_to_all(parts, ("x", "y"), 0, 0, tiled=True)
    value = jnp.sum(parts.astype(jnp.float32), axis=0).astype(jnp.bfloat16)
    value = sum_z(value)
    first_row = ((x * NY + y) * 2 + c) * CORE_ROWS
    own_scale = lax.dynamic_slice_in_dim(scale.reshape(ROWS), first_row, CORE_ROWS, 0)
    mean = value * own_scale[:, None] / (LEVELS * DEVICES)
    rotated_mean = lax.dynamic_slice_in_dim(mean, z * OWN, OWN, 0)
    grad = unrotate(mean, signs, first_row)
    grad = jnp.broadcast_to(grad[None], (PLANE, CORE_ROWS, BLK))
    grad = lax.all_to_all(grad, ("x", "y"), 0, 0, tiled=True)
    whole = place(core, grad)
    other = flip(grad, "c", 2, 1)
    grad_mean = lax.dynamic_update_slice_in_dim(whole, other[:, None], 1 - c, 1)
    return (rotated_mean, grad_mean.reshape(ROWS, BLK))


def solution(mesh):
    fine = Mesh(mesh.devices.reshape(NX, NY, 2, NZ), ("x", "y", "c", "z"))
    rows = ("x", "y", "c", "z")
    in_specs = (P(rows, None), P(rows, None), P())
    out_specs = (P(rows, None), P())
    return jax.shard_map(body, mesh=fine, in_specs=in_specs, out_specs=out_specs, check_vma=False)
```

```python
import math

import jax
import jax.numpy as jnp
import numpy as np
from jax import lax
from jax.experimental import pallas as pl
from jax.experimental.pallas import tpu as pltpu
from jax.sharding import Mesh
from jax.sharding import PartitionSpec as P

COLS = 128
BLK = 256
LEVELS = 15
BLOCKS = 56
ROWS = BLOCKS * COLS
NX = 4
NY = 4
NZ = 8
PLANE = NX * NY
DEVICES = 256
CORE_ROWS = ROWS // (2 * PLANE)
OWN = ROWS // DEVICES
GROUP = 7
STEPS = BLOCKS // GROUP
PAIRS = PLANE // STEPS
WIDTH = GROUP * BLK
AHEAD = 3
ROTATE_VMEM = 44 * 1024 * 1024
KERNEL_VMEM = 24 * 1024 * 1024
IN_VMEM = pl.BlockSpec(memory_space=pltpu.VMEM)
IN_SMEM = pl.BlockSpec(memory_space=pltpu.SMEM)
IN_ANY = pl.BlockSpec(memory_space=pl.ANY)


def hadamard(size):
    matrix = np.ones((1, 1), np.float32)
    while matrix.shape[0] < size:
        matrix = np.block([[matrix, matrix], [matrix, -matrix]])
    return matrix


HADAMARD = hadamard(BLK)


def rotate_kernel(
    core_ref,
    acts_hbm,
    cot_hbm,
    signs_hbm,
    keep_ref,
    give_ref,
    largest_ref,
    acts_ref,
    cot_ref,
    signs_ref,
    had_ref,
    cot_t,
    even_terms,
    odd_terms,
    turned_ref,
    sems,
    small_sems,
):
    core = core_ref[0]
    small = [
        pltpu.make_async_copy(source, target, small_sems.at[i])
        for i, (source, target) in enumerate(((cot_hbm, cot_ref), (signs_hbm, signs_ref)))
    ]

    def fetch(i):
        columns = pl.ds(pl.multiple_of(i * WIDTH, WIDTH), WIDTH)
        return pltpu.make_async_copy(acts_hbm.at[:, columns], acts_ref.at[i], sems.at[i])

    for copy in small:
        copy.start()
    for i in range(AHEAD):
        fetch(i).start()
    had = lax.broadcasted_iota(jnp.int32, (BLK, BLK), 0) & lax.broadcasted_iota(
        jnp.int32, (BLK, BLK), 1
    )
    for half in (4, 2, 1):
        had = had ^ (had >> half)
    had = (1 - 2 * (had & 1)).astype(jnp.float32) * (1.0 / math.sqrt(BLK))
    had = had.astype(jnp.bfloat16)
    had_ref[:BLK, :] = had
    had_ref[BLK:, :] = had
    for copy in small:
        copy.wait()
    cot_t[...] = cot_ref[...].T

    def arrive(i):
        fetch(i).wait()

        @pl.when(i + AHEAD < STEPS)
        def _():
            fetch(i + AHEAD).start()

    def multiply(i, b, terms):
        block = jnp.dot(
            cot_t[...], acts_ref[i, :, b * BLK : (b + 1) * BLK], preferred_element_type=jnp.float32
        )
        block = block * signs_ref[pl.ds(i * GROUP + b, 1), :].astype(jnp.float32)
        high = block.astype(jnp.bfloat16)
        low = (block - high.astype(jnp.float32)).astype(jnp.bfloat16)
        terms[b * COLS : (b + 1) * COLS, :BLK] = high
        terms[b * COLS : (b + 1) * COLS, BLK:] = low

    def turn(i, b, terms):
        turned = jnp.dot(
            terms[b * COLS : (b + 1) * COLS, :], had_ref[...], preferred_element_type=jnp.float32
        )
        turned_ref[b * COLS : (b + 1) * COLS, :] = turned
        size = jnp.abs(turned)
        size = jnp.maximum(size[:, :COLS], size[:, COLS:]).T
        largest_ref[pl.ds(i * GROUP + b, 1), :] = jnp.max(size, axis=0, keepdims=True)

    def hand_out(i):
        for pair in range(PAIRS):
            for ref, part in ((keep_ref, core), (give_ref, 1 - core)):
                start = pl.multiple_of((2 * pair + part) * CORE_ROWS, 8)
                ref[i * PAIRS + pair] = turned_ref[pl.ds(start, CORE_ROWS), :]

    def both(i, terms, next_terms):
        arrive(i + 1)
        for b in range(GROUP):
            multiply(i + 1, b, next_terms)
            turn(i, b, terms)
        hand_out(i)

    arrive(0)
    for b in range(GROUP):
        multiply(0, b, even_terms)

    def two_steps(k, carry):
        both(2 * k, even_terms, odd_terms)
        both(2 * k + 1, odd_terms, even_terms)
        return carry

    lax.fori_loop(0, STEPS // 2 - 1, two_steps, 0)
    both(STEPS - 2, even_terms, odd_terms)
    for b in range(GROUP):
        turn(STEPS - 1, b, odd_terms)
    hand_out(STEPS - 1)


def rotate(core, acts, cotangent, signs):
    tokens = acts.shape[0]
    half = jax.ShapeDtypeStruct((PLANE, CORE_ROWS, BLK), jnp.float32)
    return pl.pallas_call(
        rotate_kernel,
        in_specs=[IN_SMEM, IN_ANY, IN_ANY, IN_ANY],
        out_specs=[IN_VMEM, IN_VMEM, IN_VMEM],
        out_shape=[half, half, jax.ShapeDtypeStruct((BLOCKS, COLS), jnp.float32)],
        scratch_shapes=[
            pltpu.VMEM((STEPS, tokens, WIDTH), jnp.bfloat16),
            pltpu.VMEM((tokens, COLS), jnp.bfloat16),
            pltpu.VMEM((BLOCKS, BLK), jnp.int32),
            pltpu.VMEM((2 * BLK, BLK), jnp.bfloat16),
            pltpu.VMEM((COLS, tokens), jnp.bfloat16),
            pltpu.VMEM((GROUP * COLS, 2 * BLK), jnp.bfloat16),
            pltpu.VMEM((GROUP * COLS, 2 * BLK), jnp.bfloat16),
            pltpu.VMEM((GROUP * COLS, BLK), jnp.float32),
            pltpu.SemaphoreType.DMA((STEPS,)),
            pltpu.SemaphoreType.DMA((2,)),
        ],
        compiler_params=pltpu.CompilerParams(vmem_limit_bytes=ROTATE_VMEM),
        cost_estimate=pl.CostEstimate(
            flops=2 * ROWS * BLK * (tokens + 2 * BLK), bytes_accessed=17_000_000, transcendentals=0
        ),
    )(core, acts, cotangent, signs)


def quantize_kernel(core_ref, keep_ref, other_ref, scale_ref, sum_ref, factor):
    core = core_ref[0]

    def step(i, carry):
        for b in range(GROUP):
            row = LEVELS / scale_ref[pl.ds(i * GROUP + b, 1), :]
            factor[b * COLS : (b + 1) * COLS, :] = jnp.broadcast_to(row, (COLS, COLS)).T
        for pair in range(PAIRS):
            start = pl.multiple_of((2 * pair + core) * CORE_ROWS, 8)
            scale = factor[pl.ds(start, CORE_ROWS), :]
            j = i * PAIRS + pair
            for lane in (0, COLS):
                mine = jnp.floor(keep_ref[j, :, lane : lane + COLS] * scale + 0.5)
                other = jnp.floor(other_ref[j, :, lane : lane + COLS] * scale + 0.5)
                sum_ref[j, :, lane : lane + COLS] = (mine + other).astype(jnp.bfloat16)
        return carry

    lax.fori_loop(0, STEPS, step, 0, unroll=True)


def quantize(core, keep, other, scale):
    return pl.pallas_call(
        quantize_kernel,
        in_specs=[IN_SMEM, IN_VMEM, IN_VMEM, IN_VMEM],
        out_specs=IN_VMEM,
        out_shape=jax.ShapeDtypeStruct((PLANE, CORE_ROWS, BLK), jnp.bfloat16),
        scratch_shapes=[pltpu.VMEM((GROUP * COLS, COLS), jnp.float32)],
        compiler_params=pltpu.CompilerParams(vmem_limit_bytes=KERNEL_VMEM),
        cost_estimate=pl.CostEstimate(
            flops=4 * ROWS * BLK, bytes_accessed=9_200_000, transcendentals=0
        ),
    )(core, keep, other, scale)


def place_kernel(core_ref, part_ref, whole_ref, sem):
    copies = [
        pltpu.make_async_copy(part_ref.at[i], whole_ref.at[i, core_ref[0]], sem.at[i])
        for i in range(PLANE)
    ]
    for copy in copies:
        copy.start()
    for copy in copies:
        copy.wait()


def place(core, part):
    return pl.pallas_call(
        place_kernel,
        in_specs=[IN_SMEM, IN_VMEM],
        out_specs=IN_ANY,
        out_shape=jax.ShapeDtypeStruct((PLANE, 2, CORE_ROWS, BLK), jnp.bfloat16),
        scratch_shapes=[pltpu.SemaphoreType.DMA((PLANE,))],
        compiler_params=pltpu.CompilerParams(vmem_limit_bytes=KERNEL_VMEM),
        cost_estimate=pl.CostEstimate(flops=0, bytes_accessed=3_700_000, transcendentals=0),
    )(core, part)


def row_signs(signs, first_row, count):
    row_ids = first_row + jnp.arange(count, dtype=jnp.int32)
    onehot = (row_ids[:, None] // COLS == jnp.arange(BLOCKS, dtype=jnp.int32)[None, :]).astype(
        jnp.float32
    )
    return jnp.dot(onehot, signs.astype(jnp.float32), precision=lax.Precision.HIGHEST)


def unrotate(values, signs, first_row):
    back = jnp.dot(values, jnp.asarray(HADAMARD), precision=lax.Precision.HIGHEST)
    signed = back * row_signs(signs, first_row, values.shape[0])
    return (signed * (1.0 / math.sqrt(BLK))).astype(jnp.bfloat16)


def shift(value, axis, size, step):
    return lax.ppermute(value, axis, [((i + step) % size, i) for i in range(size)])


def flip(value, axis, size, bit):
    return lax.ppermute(value, axis, [(i, i ^ bit) for i in range(size)])


def mirror(value, axis, size):
    return lax.ppermute(value, axis, [(i, size - 1 - i) for i in range(size)])


def max_everywhere(value):
    for axis, size, steps in (
        ("x", NX, (1, 2, 3)),
        ("y", NY, (1, 2, 3)),
        ("z", NZ, (1, 7)),
        ("z", NZ, (3, 5)),
    ):
        got = [shift(value, axis, size, s) for s in steps]
        for g in got:
            value = jnp.maximum(value, g)
    return value


def sum_z(value):
    got = [flip(value, "z", NZ, bit) for bit in (1, 2, 3)]
    value = value.astype(jnp.float32)
    for g in got:
        value = value + g.astype(jnp.float32)
    value = value.astype(jnp.bfloat16)
    return value.astype(jnp.float32) + mirror(value, "z", NZ).astype(jnp.float32)


def body(acts, cotangent, signs):
    x, y, c, z = (lax.axis_index(a) for a in ("x", "y", "c", "z"))
    core = jnp.full((1,), c, jnp.int32)
    keep, give, largest = rotate(core, acts, cotangent, signs)
    beside = flip(largest, "c", 2, 1)
    give, beside = lax.optimization_barrier((give, beside))
    other = flip(give, "c", 2, 1)
    scale = max_everywhere(jnp.maximum(largest, beside)) + 1e-06
    parts = quantize(core, keep, other, scale)
    parts = lax.all_to_all(parts, ("x", "y"), 0, 0, tiled=True)
    value = jnp.sum(parts.astype(jnp.float32), axis=0).astype(jnp.bfloat16)
    value = sum_z(value)
    first_row = ((x * NY + y) * 2 + c) * CORE_ROWS
    own_scale = lax.dynamic_slice_in_dim(scale.reshape(ROWS), first_row, CORE_ROWS, 0)
    mean = value * own_scale[:, None] / (LEVELS * DEVICES)
    rotated_mean = lax.dynamic_slice_in_dim(mean, z * OWN, OWN, 0)
    grad = unrotate(mean, signs, first_row)
    grad = jnp.broadcast_to(grad[None], (PLANE, CORE_ROWS, BLK))
    grad = lax.all_to_all(grad, ("x", "y"), 0, 0, tiled=True)
    whole = place(core, grad)
    other = flip(grad, "c", 2, 1)
    grad_mean = lax.dynamic_update_slice_in_dim(whole, other[:, None], 1 - c, 1)
    return (rotated_mean, grad_mean.reshape(ROWS, BLK))


def solution(mesh):
    fine = Mesh(mesh.devices.reshape(NX, NY, 2, NZ), ("x", "y", "c", "z"))
    rows = ("x", "y", "c", "z")
    in_specs = (P(rows, None), P(rows, None), P())
    out_specs = (P(rows, None), P())
    return jax.shard_map(body, mesh=fine, in_specs=in_specs, out_specs=out_specs, check_vma=False)
```
